512 devices in a mesh: dp: 8 (over y, core), expert: 16 (over z), tensor: 4 (over x).
Axes of the slice: x: 4, y: 4, z: 16, core: 2. Of those that a mesh axis runs over, the one named last changes fastest.
Arguments:
- grad_out: bfloat16 [16384, 4096], P(('dp', 'expert'), 'tensor'), may hold values from -6 to 6
- tokens_in: bfloat16 [16384, 4096], P(('dp', 'expert'), 'tensor'), may hold values from -6 to 6
- router_logits: float32 [16384, 16], P(('dp', 'expert')), may hold values from -8 to 8
- expert_ids: int32 [16384, 2], P(('dp', 'expert')), may hold values from 0 to 15, as said below
- slot_index: int32 [16384, 2], P(('dp', 'expert')), may hold values from 0 to 7, as said below
- kept: int32 [16384, 2], P(('dp', 'expert')), may hold values from 0 to 1, as said below
- expert_out: bfloat16 [16384, 2, 4096], P(('dp', 'expert'), None, 'tensor'), may hold values from -0.0234375 to 0.0234375
- gate_pre: bfloat16 [16, 1024, 7168], P('expert', None, ('dp', 'tensor')), may hold values from -6 to 6
- up_pre: bfloat16 [16, 1024, 7168], P('expert', None, ('dp', 'tensor')), may hold values from -6 to 6
- down_weight: bfloat16 [16, 7168, 4096], P('expert', ('dp', 'tensor')), may hold values from -0.0625 to 0.0625
Outputs:
- gate_grad: bfloat16 [16, 1024, 7168], P('expert', None, ('dp', 'tensor'))
- up_grad: bfloat16 [16, 1024, 7168], P('expert', None, ('dp', 'tensor'))
- router_grad: float32 [16, 4096], P(None, 'tensor')
The draws below stay inside these ranges and needn't reach their ends.
Inputs may be any that keep to these rules, and one draw needn't show every extreme that they name: `expert_ids`: the two experts of a token differ. `slot_index`: for a kept route, the number of earlier routes of its group of 128 tokens to the same expert, tokens in order and a token's first route before its second; 0 for a dropped route. `kept`: 1 exactly where that number of earlier routes is below 8.
All inputs are finite; a program needn't handle non-finite values.
Results may differ from the reference program's by a relative error of at most 0.0049.
Values may be sent and summed in bfloat16 or wider, within the bound.
A program may use at most 64 MiB of HBM per device.

```python
import jax
import jax.numpy as jnp
from jax import lax

D = 4096
FFW = 7168
TOP = 2
TOK_DEV = 128
EXPERTS = 16
TOKENS = 16384
CAP = 8
CQ = 2
SLOTS = 1024
N_EXPERT = 16
N_TENSOR = 4


def route_tables(key):
    keys = jax.random.split(key, 6)
    hot_expert = jax.random.randint(keys[0], (), 0, EXPERTS)
    offset_id = jax.random.randint(keys[1], (), 0, EXPERTS)
    left_draw = jax.random.randint(keys[2], (TOKENS,), 0, EXPERTS)
    right_draw = jax.random.randint(keys[3], (TOKENS,), 0, EXPERTS)
    leading = (left_draw * right_draw // EXPERTS + offset_id) % EXPERTS
    start_pos = jax.random.randint(keys[4], (TOKENS // TOK_DEV, 1), 0, TOK_DEV)
    position = (jnp.arange(TOKENS, dtype=jnp.int32).reshape(TOKENS // TOK_DEV, TOK_DEV) - start_pos) % TOK_DEV
    leading = jnp.where(position.reshape(-1) < CAP, hot_expert, leading)
    trailing = (leading + 1 + jax.random.randint(keys[5], (TOKENS,), 0, EXPERTS - 1)) % EXPERTS
    route_ids = jnp.stack([leading, trailing], axis=1).astype(jnp.int32)
    member = (route_ids.reshape(TOKENS // TOK_DEV, TOK_DEV * TOP)[:, :, None] == jnp.arange(EXPERTS, dtype=jnp.int32)[None, None, :]).astype(jnp.int32)
    before = jnp.cumsum(member, axis=1) - member
    position_all = jnp.sum(before * member, axis=2).reshape(TOKENS, TOP).astype(jnp.int32)
    keep_flag = (position_all < CAP).astype(jnp.int32)
    slot_vals = jnp.where(keep_flag == 1, position_all, 0).astype(jnp.int32)
    return (route_ids, slot_vals, keep_flag)


def draw_expert_ids(key, part):
    tables = route_tables(key)
    return tables[0]


def draw_slot_index(key, part):
    tables = route_tables(key)
    return tables[1]


def draw_kept(key, part):
    tables = route_tables(key)
    return tables[2]


def block_scale(key, shape, cuts, least, high):
    loudness, own = 1.0, jax.random.fold_in(key, 6)
    for dim, parts in cuts:
        steps = jnp.exp(jax.random.uniform(jax.random.fold_in(own, dim), (parts,), jnp.float32, least / len(cuts), high / len(cuts)))
        loudness = loudness * jnp.repeat(steps, shape[dim] // parts).reshape([-1 if axis == dim else 1 for axis in range(len(shape))])
    return loudness


def noise(rng, shape, scale, most, cuts=(), kind=jnp.bfloat16):
    drawn = jax.random.normal(rng, shape, jnp.float32) * scale
    if len(cuts) > 0:
        drawn = block_scale(rng, shape, cuts, -0.22, 0.18) * drawn
    return jnp.clip(drawn, min=-most, max=most).astype(kind)


def setup_inputs(seed: int = 0) -> dict:
    splits = jax.random.split(jax.random.key(seed), 11)
    grad_out = noise(splits[0], (TOKENS, D), 1.0, 6.0, ((0, 128), (1, 4)))
    tokens_in = noise(splits[1], (TOKENS, D), 1.0, 6.0, ((0, 128), (1, 4)))
    router_logits = noise(splits[2], (TOKENS, EXPERTS), 1.5, 8.0, ((0, 128),), jnp.float32)
    expert_ids = draw_expert_ids(jax.random.fold_in(splits[10], 71), 0)
    slot_index = draw_slot_index(jax.random.fold_in(splits[10], 71), 0)
    kept = draw_kept(jax.random.fold_in(splits[10], 71), 0)
    expert_out = noise(splits[6], (TOKENS, TOP, D), 0.0015, 0.0234375, ((0, 128), (2, 4)))
    gate_pre = noise(splits[7], (EXPERTS, SLOTS, FFW), 1.0, 6.0, ((0, 16), (2, 32)))
    up_pre = noise(splits[8], (EXPERTS, SLOTS, FFW), 1.0, 6.0, ((0, 16), (2, 32)))
    down_weight = noise(splits[9], (EXPERTS, FFW, D), FFW ** -0.5, 0.0625, ((0, 16), (1, 32)))
    return {"grad_out": grad_out, "tokens_in": tokens_in, "router_logits": router_logits, "expert_ids": expert_ids, "slot_index": slot_index, "kept": kept, "expert_out": expert_out, "gate_pre": gate_pre, "up_pre": up_pre, "down_weight": down_weight}


def project_expert(operands):
    return lax.dot_general(operands[0], operands[1], (((1,), (1,)), ((), ())), preferred_element_type=jnp.float32)


def reference(grad_out, tokens_in, router_logits, expert_ids, slot_index, kept, expert_out, gate_pre, up_pre, down_weight):
    onehot = (expert_ids[:, :, None] == jnp.arange(EXPERTS, dtype=jnp.int32)[None, None, :]).astype(jnp.float32)
    chosen = jnp.sum(onehot * router_logits[:, None, :], axis=2)
    prob_first = jax.nn.sigmoid(chosen[:, 0] - chosen[:, 1])
    prob_second = 1.0 - prob_first
    weights = jnp.stack([prob_first, prob_second], axis=1)
    keep_float = kept.astype(jnp.float32)
    scaled = ((weights * keep_float)[:, :, None] * grad_out.astype(jnp.float32)[:, None, :]).astype(jnp.bfloat16)
    group_ids = (jnp.arange(TOKENS, dtype=jnp.int32) // TOK_DEV).astype(jnp.int32)
    row_dp = group_ids // N_EXPERT
    row_src = group_ids % N_EXPERT
    slot_row = ((row_dp[:, None] * N_TENSOR + slot_index // CQ) * N_EXPERT + row_src[:, None]) * CQ + slot_index % CQ
    flat_rows = (expert_ids * SLOTS + slot_row).astype(jnp.int32).reshape(-1)
    routed = jnp.zeros((EXPERTS * SLOTS, D), jnp.float32)
    routed = routed.at[flat_rows].add(scaled.reshape(-1, D).astype(jnp.float32))
    routed = routed.astype(jnp.bfloat16).reshape(EXPERTS, SLOTS, D)
    hidden_grad = lax.map(project_expert, (routed, down_weight))
    gate_vals = gate_pre.astype(jnp.float32)
    sigma_gate = jax.nn.sigmoid(gate_vals)
    up_grad = (hidden_grad * gate_vals * sigma_gate).astype(jnp.bfloat16)
    gate_grad = (hidden_grad * up_pre.astype(jnp.float32) * sigma_gate * (1.0 + gate_vals * (1.0 - sigma_gate))).astype(jnp.bfloat16)
    scores = jnp.sum(grad_out.astype(jnp.float32)[:, None, :] * expert_out.astype(jnp.float32), axis=2) * keep_float
    coefficient = prob_first * prob_second * (scores[:, 0] - scores[:, 1])
    logit_grad = coefficient[:, None] * (onehot[:, 0, :] - onehot[:, 1, :])
    router_grad = jnp.dot(logit_grad.T, tokens_in.astype(jnp.float32), precision=lax.Precision.HIGHEST)
    return gate_grad, up_grad, router_grad
```

```python
import functools

import jax
import jax.numpy as jnp
from jax import lax
from jax.experimental import pallas as pl
from jax.experimental.pallas import tpu as pltpu
from jax.sharding import PartitionSpec as P

MESH = pl.DeviceIdType.MESH
F32 = jnp.float32
BF16 = jnp.bfloat16

NZ = 16
NX = 4
NY = 4
NJ = 2
HID = 224
HALF = 512
ROWS = 64

OWN, MINUS, PLUS, OPP = 0, 1, 2, 3


def kernel(
    g_hbm, tok_hbm, eo_hbm, gate_hbm, up_hbm, w_hbm, logits_ref, ids_ref, slot_ref, kept_ref,
    gg_hbm, ug_hbm, rg_ref,
    g, tok, eo, gate, up, wbuf, fac_u, fac_g, out_u, out_g,
    tx, rx_same, rx_cross, rows, p_own, p_tx, p_rx,
    sc_tx, sc_rx, rt, r1, r2, r3,
    in_sem, w_sem, wr_sem, z_send, z_recv, a_send, a_recv, p_send, p_recv,
    sc_send, sc_recv, r_send, r_recv, o_sem,
):
    dp = lax.axis_index("dp")
    z = lax.axis_index("expert")
    x = lax.axis_index("tensor")
    y = dp // 2
    c = dp % 2
    partner = dp + 1 - 2 * c
    xs = [x, (x + 3) % 4, (x + 1) % 4, (x + 2) % 4]
    ys = [y, (y + 3) % 4, (y + 1) % 4, (y + 2) % 4]

    def fetch(i, src, dst):
        copy = pltpu.make_async_copy(src, dst, in_sem.at[i])
        copy.start()
        return copy

    cp_g = fetch(0, g_hbm, g)
    cp_eo = fetch(1, eo_hbm, eo)
    cp_tok = fetch(2, tok_hbm, tok)
    cp_gate = fetch(3, gate_hbm.at[0], gate)
    cp_up = fetch(4, up_hbm.at[0], up)
    for q in range(NX):
        pltpu.make_async_copy(
            w_hbm.at[0, :, pl.ds(pl.multiple_of(q * 1024 + c * HALF, HALF), HALF)],
            wbuf.at[0, q],
            w_sem.at[0],
        ).start()

    barrier = pltpu.get_barrier_semaphore()

    def greet(**where):
        pl.semaphore_signal(barrier, inc=1, device_id=where, device_id_type=MESH)

    for k in range(1, NZ):
        greet(expert=(z + k) % NZ)
        greet(expert=(z + k) % NZ, dp=partner)
    for k in range(1, NX):
        greet(tensor=(x + k) % NX)
    for k in range(1, 2 * NY):
        greet(dp=(dp + k) % (2 * NY))

    ids = ids_ref[...]
    slots = slot_ref[...]
    kept = kept_ref[...]
    logits = logits_ref[...]
    expert_row = lax.broadcasted_iota(jnp.int32, (16, 128), 0)
    hot = [(expert_row == ids[k : k + 1, :]).astype(F32) for k in range(2)]
    chosen = [jnp.sum(hot[k] * logits, axis=0, keepdims=True) for k in range(2)]
    w0 = 1.0 / (1.0 + jnp.exp(chosen[1] - chosen[0]))
    wts = [w0, 1.0 - w0]
    keep = [kept[k : k + 1, :].astype(F32) for k in range(2)]

    row = lax.broadcasted_iota(jnp.int32, (256, 128), 0)
    row_key = (row // 16) * 4 + row % 4
    row_blk = (row // 4) % 4
    sel = []
    for j in range(NJ):
        one = jnp.zeros((256, 128), F32)
        val = jnp.zeros((256, 128), F32)
        for k in range(2):
            s = slots[k : k + 1, :]
            mine = jnp.logical_and(kept[k : k + 1, :] == 1, s // 4 == j)
            key = jnp.where(mine, ids[k : k + 1, :] * 4 + s % 4, -1)
            hit = (row_key == key).astype(F32)
            one = one + hit
            val = val + hit * wts[k]
        scale = jnp.sum(val, axis=1, keepdims=True)
        wide = jnp.concatenate(
            [jnp.where(row_blk == f, one, 0.0).astype(BF16) for f in range(4)], axis=1
        )
        sel.append((wide, scale))
    cp_g.wait()
    for h in range(2):
        tall = jnp.concatenate(
            [g[:, h * HALF + f * 128 : h * HALF + (f + 1) * 128] for f in range(4)], axis=0
        )
        for j in range(NJ):
            wide, scale = sel[j]
            picked = jnp.dot(wide, tall, preferred_element_type=F32)
            tx[j, h * NZ : (h + 1) * NZ] = (picked * scale).astype(BF16).reshape(NZ, 16, 128)

    pl.semaphore_wait(barrier, 2 * (NZ - 1) + (NX - 1) + (2 * NY - 1))

    order = []
    for k in range(1, NZ // 2):
        order += [k, NZ - k]
    order.append(NZ // 2)
    for j in range(NJ):
        for k in [0] + order:
            to = (z + k) % NZ
            pltpu.make_async_remote_copy(
                src_ref=tx.at[j, (1 - c) * NZ + to],
                dst_ref=rx_cross.at[j, k],
                send_sem=z_send.at[j],
                recv_sem=z_recv.at[j, 1],
                device_id={"expert": to, "dp": partner},
                device_id_type=MESH,
            ).start()
            if k > 0:
                pltpu.make_async_remote_copy(
                    src_ref=tx.at[j, c * NZ + to],
                    dst_ref=rx_same.at[j, k],
                    send_sem=z_send.at[j],
                    recv_sem=z_recv.at[j, 0],
                    device_id={"expert": to},
                    device_id_type=MESH,
                ).start()
        rx_same[j, 0] = tx[j, c * NZ + z]

    for q in range(NX):
        pltpu.make_async_remote_copy(
            src_ref=w_hbm.at[0, :, pl.ds(pl.multiple_of(q * 1024 + (1 - c) * HALF, HALF), HALF)],
            dst_ref=wbuf.at[1, q],
            send_sem=wr_sem.at[0],
            recv_sem=wr_sem.at[1],
            device_id={"dp": partner},
            device_id_type=MESH,
        ).start()

    cp_eo.wait()
    parts = [jnp.zeros((128, 128), F32) for _ in range(2)]
    for f in range(8):
        cols = slice(f * 128, (f + 1) * 128)
        grad = g[:, cols].astype(F32)
        both = eo[:, :, cols].astype(F32)
        for k in range(2):
            parts[k] = parts[k] + grad * both[:, k, :]
    score = [jnp.sum(parts[k].T, axis=0, keepdims=True) for k in range(2)]
    sub = lax.broadcasted_iota(jnp.int32, (8, 128), 0)
    sc_tx[...] = jnp.where(sub == 0, score[0], jnp.where(sub == 1, score[1], 0.0))
    for k in range(1, NX):
        pltpu.make_async_remote_copy(
            src_ref=sc_tx,
            dst_ref=sc_rx.at[k - 1],
            send_sem=sc_send.at[k - 1],
            recv_sem=sc_recv.at[k - 1],
            device_id={"tensor": (x + k) % NX},
            device_id_type=MESH,
        ).start()

    cp_gate.wait()
    cp_up.wait()
    for i in range(8):
        part = slice(i * 128, (i + 1) * 128)
        a = gate[part, :].astype(F32)
        b = up[part, :].astype(F32)
        sigma = 1.0 / (1.0 + jnp.exp(-a))
        fac_u[part, :] = a * sigma
        fac_g[part, :] = b * sigma * (1.0 + a * (1.0 - sigma))

    def place(ch, first, second):
        if ch == 0:
            return xs[first] * 4 + ys[second]
        return xs[second] * 4 + ys[first]

    def push(ch, j, first, second, along_first, way, part, slot):
        axis_x = along_first == (ch == 0)
        if axis_x:
            where = {"tensor": xs[way]}
        else:
            where = {"dp": ys[way] * 2 + c}
        ref = rows.at[ch, j, place(ch, first, second)]
        if part is not None:
            ref = ref.at[pl.ds(part * 32, 32)]
        pltpu.make_async_remote_copy(
            src_ref=ref,
            dst_ref=ref,
            send_sem=a_send.at[ch, j],
            recv_sem=a_recv.at[ch, j, slot],
            device_id=where,
            device_id_type=MESH,
        ).start()

    def arrived(ch, j, first, second, part, slot):
        ref = rows.at[ch, j, place(ch, first, second)]
        if part is not None:
            ref = ref.at[pl.ds(part * 32, 32)]
        pltpu.make_async_copy(ref, ref, a_recv.at[ch, j, slot]).wait()

    def spread(ch, j, first):
        push(ch, j, first, OWN, False, PLUS, None, 4 + 4 * first)
        push(ch, j, first, OWN, False, MINUS, None, 5 + 4 * first)

    def step_a(ch, j):
        push(ch, j, OWN, OWN, True, PLUS, None, 0)
        push(ch, j, OWN, OWN, True, MINUS, None, 1)
        spread(ch, j, OWN)

    def step_b(ch, j):
        arrived(ch, j, MINUS, OWN, None, 0)
        push(ch, j, MINUS, OWN, True, PLUS, 0, 2)
        spread(ch, j, MINUS)
        arrived(ch, j, PLUS, OWN, None, 1)
        push(ch, j, PLUS, OWN, True, MINUS, 1, 3)
        spread(ch, j, PLUS)

    def step_c(ch, j):
        arrived(ch, j, OPP, OWN, 0, 2)
        arrived(ch, j, OPP, OWN, 1, 3)
        spread(ch, j, OPP)

    def step_d(ch, j, first):
        arrived(ch, j, first, MINUS, None, 4 + 4 * first)
        push(ch, j, first, MINUS, False, PLUS, 0, 6 + 4 * first)
        arrived(ch, j, first, PLUS, None, 5 + 4 * first)
        push(ch, j, first, PLUS, False, MINUS, 1, 7 + 4 * first)

    def step_e(ch, j, first):
        arrived(ch, j, first, OPP, 0, 6 + 4 * first)
        arrived(ch, j, first, OPP, 1, 7 + 4 * first)

    out_row = lax.broadcasted_iota(jnp.int32, (256, 256), 0)
    in_row = lax.broadcasted_iota(jnp.int32, (256, 256), 1)
    src = (z + NZ - (out_row // 2) % 16) % NZ
    want = src * 16 + (out_row // 64) * 4 + ((out_row // 32) % 2) * 2 + out_row % 2
    perm = (in_row == want).astype(BF16)

    def unpack(j):
        pltpu.make_async_copy(rx_same.at[j, pl.ds(1, 15)], rx_same.at[j, pl.ds(1, 15)], z_recv.at[j, 0]).wait()
        pltpu.make_async_copy(rx_cross.at[j], rx_cross.at[j], z_recv.at[j, 1]).wait()
        for ch, ref in ((0, rx_same), (1, rx_cross)):
            out = jnp.dot(perm, ref[j].reshape(256, 128), preferred_element_type=F32).astype(BF16)
            for f in range(4):
                rows[ch, j, place(ch, OWN, OWN), :, f * 128 : (f + 1) * 128] = out[f * 64 : (f + 1) * 64]
            step_a(ch, j)

    def matmul(ch, j, rel):
        total = [None, None]
        for q in range(NX):
            block = rows[ch, j, q * 4 + ys[rel]]
            for side in (0, 1):
                term = lax.dot_general(
                    block, wbuf[side, q], (((1,), (1,)), ((), ())), preferred_element_type=F32
                )
                total[side] = term if total[side] is None else total[side] + term
        p_tx[ch, j, rel] = total[1]
        pltpu.make_async_remote_copy(
            src_ref=p_tx.at[ch, j, rel],
            dst_ref=p_rx.at[1 - ch, j, rel],
            send_sem=p_send.at[ch, j, rel],
            recv_sem=p_recv.at[1 - ch, j, rel],
            device_id={"dp": partner},
            device_id_type=MESH,
        ).start()
        p_own[ch, j, rel] = total[0]

    def finish(ch, j, rel):
        pltpu.make_async_copy(p_rx.at[ch, j, rel], p_rx.at[ch, j, rel], p_recv.at[ch, j, rel]).wait()
        hidden = p_own[ch, j, rel] + p_rx[ch, j, rel]
        core = c if ch == 0 else 1 - c
        at = pl.ds(pl.multiple_of((ys[rel] * 2 + core) * 128 + j * ROWS, ROWS), ROWS)
        out_u[at, :] = (hidden * fac_u[at, :]).astype(BF16)
        out_g[at, :] = (hidden * fac_g[at, :]).astype(BF16)
        pltpu.make_async_copy(out_u.at[at], ug_hbm.at[0, at], o_sem.at[0]).start()
        pltpu.make_async_copy(out_g.at[at], gg_hbm.at[0, at], o_sem.at[1]).start()

    def router_a():
        for k in range(1, NX):
            pltpu.make_async_copy(sc_rx.at[k - 1], sc_rx.at[k - 1], sc_recv.at[k - 1]).wait()
        total = sc_tx[...] + sc_rx[0] + sc_rx[1] + sc_rx[2]
        diff = total[0:1, :] * keep[0] - total[1:2, :] * keep[1]
        coef = wts[0] * wts[1] * diff
        logit_grad = coef * (hot[0] - hot[1])
        high = logit_grad.astype(BF16)
        rest = logit_grad - high.astype(F32)
        mid = rest.astype(BF16)
        low = (rest - mid.astype(F32)).astype(BF16)
        cp_tok.wait()
        terms = jnp.dot(
            jnp.concatenate([high, mid, low], axis=0), tok[...], preferred_element_type=F32
        )
        term = terms[0:16] + terms[16:32] + terms[32:48]
        for p in range(16):
            rt[p] = term[(p // 8) * 8 : (p // 8) * 8 + 8, (p % 8) * 128 : (p % 8) * 128 + 128]
        for k in range(1, NZ):
            to = (z + k) % NZ
            pltpu.make_async_remote_copy(
                src_ref=rt.at[to],
                dst_ref=r1.at[k - 1],
                send_sem=r_send.at[0],
                recv_sem=r_recv.at[0],
                device_id={"expert": to},
                device_id_type=MESH,
            ).start()

    def router_b():
        pltpu.make_async_copy(r1, r1, r_recv.at[0]).wait()
        total = rt[z]
        for k in range(NZ - 1):
            total = total + r1[k]
        r2[dp] = total
        for k in range(1, 2 * NY):
            pltpu.make_async_remote_copy(
                src_ref=r2.at[dp],
                dst_ref=r2.at[dp],
                send_sem=r_send.at[1],
                recv_sem=r_recv.at[1],
                device_id={"dp": (dp + k) % (2 * NY)},
                device_id_type=MESH,
            ).start()

    def router_c():
        pltpu.make_async_copy(r2.at[pl.ds(0, 7)], r2.at[pl.ds(0, 7)], r_recv.at[1]).wait()
        total = r2[0]
        for k in range(1, 2 * NY):
            total = total + r2[k]
        r3[z] = total
        for k in range(1, NZ):
            pltpu.make_async_remote_copy(
                src_ref=r3.at[z],
                dst_ref=r3.at[z],
                send_sem=r_send.at[2],
                recv_sem=r_recv.at[2],
                device_id={"expert": (z + k) % NZ},
                device_id_type=MESH,
            ).start()

    def router_d():
        pltpu.make_async_copy(r3.at[pl.ds(0, 15)], r3.at[pl.ds(0, 15)], r_recv.at[2]).wait()
        for p in range(16):
            rg_ref[(p // 8) * 8 : (p // 8) * 8 + 8, (p % 8) * 128 : (p % 8) * 128 + 128] = r3[p]

    unpack(0)
    router_a()
    step_b(0, 0)
    step_b(1, 0)
    unpack(1)
    step_c(0, 0)
    step_c(1, 0)
    step_d(0, 0, OWN)
    step_d(1, 0, OWN)
    step_b(0, 1)
    step_b(1, 1)
    router_b()
    pltpu.make_async_copy(wbuf.at[0], wbuf.at[0], w_sem.at[0]).wait()
    pltpu.make_async_copy(wbuf.at[1], wbuf.at[1], wr_sem.at[1]).wait()
    matmul(0, 0, OWN)
    step_d(0, 0, MINUS)
    step_d(1, 0, MINUS)
    step_c(0, 1)
    step_c(1, 1)
    step_d(0, 0, PLUS)
    step_d(1, 0, PLUS)
    step_d(0, 0, OPP)
    step_d(1, 0, OPP)
    step_e(1, 0, OWN)
    matmul(1, 0, OWN)
    finish(0, 0, OWN)
    matmul(0, 0, MINUS)
    step_d(0, 1, OWN)
    step_d(1, 1, OWN)
    finish(1, 0, OWN)
    matmul(0, 0, PLUS)
    router_c()
    matmul(0, 1, OWN)
    step_d(0, 1, MINUS)
    step_d(1, 1, MINUS)
    for first in (MINUS, PLUS):
        step_e(1, 0, first)
        matmul(1, 0, first)
        finish(0, 0, first)
    step_d(0, 1, PLUS)
    step_d(1, 1, PLUS)
    for first in range(4):
        step_e(0, 0, first)
    step_e(1, 0, OPP)
    matmul(0, 0, OPP)
    matmul(1, 0, OPP)
    step_d(0, 1, OPP)
    step_d(1, 1, OPP)
    finish(1, 0, MINUS)
    finish(1, 0, PLUS)
    step_e(1, 1, OWN)
    matmul(1, 1, OWN)
    matmul(0, 1, MINUS)
    matmul(0, 1, PLUS)
    finish(0, 0, OPP)
    finish(1, 0, OPP)
    finish(0, 1, OWN)
    router_d()
    for first in (MINUS, PLUS):
        step_e(1, 1, first)
        matmul(1, 1, first)
        finish(0, 1, first)
    finish(1, 1, OWN)
    finish(1, 1, MINUS)
    for first in range(4):
        step_e(0, 1, first)
    matmul(0, 1, OPP)
    step_e(1, 1, OPP)
    matmul(1, 1, OPP)
    finish(1, 1, PLUS)

    for j in range(NJ):
        pltpu.make_async_copy(tx.at[j, pl.ds(0, 31)], tx.at[j, pl.ds(0, 31)], z_send.at[j]).wait()
        for ch in range(2):
            sent = rows.at[ch, j, pl.ds(0, 15)]
            pltpu.make_async_copy(sent, sent, a_send.at[ch, j]).wait()
            for rel in range(NY):
                sent = p_tx.at[ch, j, rel]
                pltpu.make_async_copy(sent, sent, p_send.at[ch, j, rel]).wait()
    for k in range(NX - 1):
        pltpu.make_async_copy(sc_tx, sc_tx, sc_send.at[k]).wait()
    pltpu.make_async_copy(wbuf.at[1], wbuf.at[1], wr_sem.at[0]).wait()
    pltpu.make_async_copy(r1, r1, r_send.at[0]).wait()
    pltpu.make_async_copy(r2.at[pl.ds(0, 7)], r2.at[pl.ds(0, 7)], r_send.at[1]).wait()
    pltpu.make_async_copy(r1, r1, r_send.at[2]).wait()
    finish(0, 1, OPP)
    finish(1, 1, OPP)
    pltpu.make_async_copy(out_u, ug_hbm.at[0], o_sem.at[0]).wait()
    pltpu.make_async_copy(out_g, gg_hbm.at[0], o_sem.at[1]).wait()


def body(
    grad_out,
    tokens_in,
    router_logits,
    expert_ids,
    slot_index,
    kept,
    expert_out,
    gate_pre,
    up_pre,
    down_weight,
):
    anywhere = pl.BlockSpec(memory_space=pl.ANY)
    vmem = pl.BlockSpec(memory_space=pltpu.VMEM)
    dma = pltpu.SemaphoreType.DMA
    slots = gate_pre.shape[1]
    return pl.pallas_call(
        kernel,
        out_shape=(
            jax.ShapeDtypeStruct(gate_pre.shape, BF16),
            jax.ShapeDtypeStruct(gate_pre.shape, BF16),
            jax.ShapeDtypeStruct((16, 1024), F32),
        ),
        in_specs=[anywhere] * 6 + [vmem] * 4,
        out_specs=(anywhere, anywhere, vmem),
        scratch_shapes=[
            pltpu.VMEM((128, 1024), BF16),
            pltpu.VMEM((128, 1024), BF16),
            pltpu.VMEM((128, 2, 1024), BF16),
            pltpu.VMEM((slots, HID), BF16),
            pltpu.VMEM((slots, HID), BF16),
            pltpu.VMEM((2, NX, HID, HALF), BF16),
            pltpu.VMEM((slots, HID), F32),
            pltpu.VMEM((slots, HID), F32),
            pltpu.VMEM((slots, HID), BF16),
            pltpu.VMEM((slots, HID), BF16),
            pltpu.VMEM((NJ, 2 * NZ, 16, 128), BF16),
            pltpu.VMEM((NJ, NZ, 16, 128), BF16),
            pltpu.VMEM((NJ, NZ, 16, 128), BF16),
            pltpu.VMEM((2, NJ, NX * NY, ROWS, HALF), BF16),
            pltpu.VMEM((2, NJ, NY, ROWS, HID), F32),
            pltpu.VMEM((2, NJ, NY, ROWS, HID), F32),
            pltpu.VMEM((2, NJ, NY, ROWS, HID), F32),
            pltpu.VMEM((8, 128), F32),
            pltpu.VMEM((NX - 1, 8, 128), F32),
            pltpu.VMEM((NZ, 8, 128), F32),
            pltpu.VMEM((NZ - 1, 8, 128), F32),
            pltpu.VMEM((2 * NY, 8, 128), F32),
            pltpu.VMEM((NZ, 8, 128), F32),
            dma((5,)),
            dma((1,)),
            dma((2,)),
            dma((NJ,)),
            dma((NJ, 2)),
            dma((2, NJ)),
            dma((2, NJ, 20)),
            dma((2, NJ, NY)),
            dma((2, NJ, NY)),
            dma((NX - 1,)),
            dma((NX - 1,)),
            dma((3,)),
            dma((3,)),
            dma((2,)),
        ],
        compiler_params=pltpu.CompilerParams(
            collective_id=0, has_side_effects=True, vmem_limit_bytes=48 * 1024 * 1024
        ),
    )(
        grad_out,
        tokens_in,
        expert_out,
        gate_pre,
        up_pre,
        down_weight,
        router_logits.T,
        expert_ids.T,
        slot_index.T,
        kept.T,
    )


def solution(mesh):
    in_specs = (
        P(("dp", "expert"), "tensor"),
        P(("dp", "expert"), "tensor"),
        P(("dp", "expert"), None),
        P(("dp", "expert"), None),
        P(("dp", "expert"), None),
        P(("dp", "expert"), None),
        P(("dp", "expert"), None, "tensor"),
        P("expert", None, ("dp", "tensor")),
        P("expert", None, ("dp", "tensor")),
        P("expert", ("dp", "tensor"), None),
    )
    out_specs = (
        P("expert", None, ("dp", "tensor")),
        P("expert", None, ("dp", "tensor")),
        P(None, "tensor"),
    )
    return jax.shard_map(body, mesh=mesh, in_specs=in_specs, out_specs=out_specs, check_vma=False)
```

```python
import functools

import jax
import jax.numpy as jnp
from jax import lax
from jax.experimental import pallas as pl
from jax.experimental.pallas import tpu as pltpu
from jax.sharding import PartitionSpec as P

MESH = pl.DeviceIdType.MESH
F32 = jnp.float32
BF16 = jnp.bfloat16

NZ = 16
NX = 4
NY = 4
NJ = 2
HID = 224
HALF = 512
ROWS = 128
PART = HALF // NJ

DISPATCH = True
GATHER = True
MATMUL = True
ROUTER = True

OWN, MINUS, PLUS, OPP = 0, 1, 2, 3


def kernel(
    g_hbm, tok_hbm, eo_hbm, gate_hbm, up_hbm, w_hbm, logits_hbm, ids_hbm, slot_hbm, kept_hbm,
    gg_ref, ug_ref, rg_ref,
    g, tok, eo, gate, up, logits_ref, ids_ref, slot_ref, kept_ref, wbuf, fac_u, fac_g,
    tx, rx_same, rx_cross, rows, p_own, p_tx, p_rx,
    sc_tx, sc_rx, rt, r1, r2, r3,
    in_sem, w_sem, wr_sem, z_send, z_recv, a_send, a_recv, p_send, p_recv,
    sc_send, sc_recv, r_send, r_recv,
):
    dp = lax.axis_index("dp")
    z = lax.axis_index("expert")
    x = lax.axis_index("tensor")
    y = dp // 2
    c = dp % 2
    partner = dp + 1 - 2 * c
    xs = [x, (x + 3) % 4, (x + 1) % 4, (x + 2) % 4]
    ys = [y, (y + 3) % 4, (y + 1) % 4, (y + 2) % 4]

    def fetch(i, src, dst):
        copy = pltpu.make_async_copy(src, dst, in_sem.at[i])
        copy.start()
        return copy

    routes = [
        fetch(5, logits_hbm, logits_ref),
        fetch(6, ids_hbm, ids_ref),
        fetch(7, slot_hbm, slot_ref),
        fetch(8, kept_hbm, kept_ref),
    ]
    cp_g = fetch(0, g_hbm, g)

    barrier = pltpu.get_barrier_semaphore()

    def greet(**where):
        pl.semaphore_signal(barrier, inc=1, device_id=where, device_id_type=MESH)

    far_first = [NZ // 2]
    for k in range(NZ // 2 - 1, 0, -1):
        far_first += [k, NZ - k]
    for k in far_first:
        greet(expert=(z + k) % NZ)
        greet(expert=(z + k) % NZ, dp=partner)
    for k in range(1, NX):
        greet(tensor=(x + k) % NX)
    for k in range(1, 2 * NY):
        greet(dp=(dp + k) % (2 * NY))

    cp_eo = fetch(1, eo_hbm, eo)
    cp_tok = fetch(2, tok_hbm, tok)
    cp_gate = fetch(3, gate_hbm.at[0], gate)
    cp_up = fetch(4, up_hbm.at[0], up)
    for q in range(NX):
        pltpu.make_async_copy(
            w_hbm.at[0, :, pl.ds(pl.multiple_of(q * 1024 + c * HALF, HALF), HALF)],
            wbuf.at[0, q],
            w_sem.at[0],
        ).start()

    for copy in routes:
        copy.wait()
    ids = ids_ref[...]
    slots = slot_ref[...]
    kept = kept_ref[...]
    logits = logits_ref[...]
    expert_row = lax.broadcasted_iota(jnp.int32, (16, 128), 0)
    hot = [(expert_row == ids[k : k + 1, :]).astype(F32) for k in range(2)]
    chosen = [jnp.sum(hot[k] * logits, axis=0, keepdims=True) for k in range(2)]
    w0 = 1.0 / (1.0 + jnp.exp(chosen[1] - chosen[0]))
    wts = [w0, 1.0 - w0]
    keep = [kept[k : k + 1, :].astype(F32) for k in range(2)]

    row = lax.broadcasted_iota(jnp.int32, (256, 128), 0)
    row_key = (row // 16) * 8 + row % 8
    row_blk = (row // 8) % 2
    one = jnp.zeros((256, 128), F32)
    val = jnp.zeros((256, 128), F32)
    for k in range(2):
        key = jnp.where(kept[k : k + 1, :] == 1, ids[k : k + 1, :] * 8 + slots[k : k + 1, :], -1)
        hit = (row_key == key).astype(F32)
        one = one + hit
        val = val + hit * wts[k]
    scale = jnp.sum(val, axis=1, keepdims=True)
    wide = jnp.concatenate(
        [jnp.where(row_blk == f, one, 0.0).astype(BF16) for f in range(2)], axis=1
    )
    cp_g.wait()
    for j in range(NJ):
        for h in range(2):
            at = h * HALF + j * PART
            tall = jnp.concatenate([g[:, at : at + 128], g[:, at + 128 : at + 256]], axis=0)
            picked = jnp.dot(wide, tall, preferred_element_type=F32)
            tx[j, h * NZ : (h + 1) * NZ] = (picked * scale).astype(BF16).reshape(NZ, 16, 128)

    pl.semaphore_wait(barrier, 2 * (NZ - 1) + (NX - 1) + (2 * NY - 1))

    for j in range(NJ if DISPATCH else 0):
        rx_same[j, 0] = tx[j, c * NZ + z]
        for k in far_first:
            to = (z + k) % NZ
            pltpu.make_async_remote_copy(
                src_ref=tx.at[j, c * NZ + to],
                dst_ref=rx_same.at[j, k],
                send_sem=z_send.at[j],
                recv_sem=z_recv.at[j, 0],
                device_id={"expert": to},
                device_id_type=MESH,
            ).start()
        for k in far_first + [0]:
            to = (z + k) % NZ
            pltpu.make_async_remote_copy(
                src_ref=tx.at[j, (1 - c) * NZ + to],
                dst_ref=rx_cross.at[j, k],
                send_sem=z_send.at[j],
                recv_sem=z_recv.at[j, 1],
                device_id={"expert": to, "dp": partner},
                device_id_type=MESH,
            ).start()

    for q in range(NX):
        pltpu.make_async_remote_copy(
            src_ref=w_hbm.at[0, :, pl.ds(pl.multiple_of(q * 1024 + (1 - c) * HALF, HALF), HALF)],
            dst_ref=wbuf.at[1, q],
            send_sem=wr_sem.at[0],
            recv_sem=wr_sem.at[1],
            device_id={"dp": partner},
            device_id_type=MESH,
        ).start()

    cp_eo.wait()
    parts = [jnp.zeros((128, 128), F32) for _ in range(2)]
    for f in range(8):
        cols = slice(f * 128, (f + 1) * 128)
        grad = g[:, cols].astype(F32)
        both = eo[:, :, cols].astype(F32)
        for k in range(2):
            parts[k] = parts[k] + grad * both[:, k, :]
    score = [jnp.sum(parts[k].T, axis=0, keepdims=True) for k in range(2)]
    sub = lax.broadcasted_iota(jnp.int32, (8, 128), 0)
    sc_tx[...] = jnp.where(sub == 0, score[0], jnp.where(sub == 1, score[1], 0.0))
    for k in range(1, NX if ROUTER else 1):
        pltpu.make_async_remote_copy(
            src_ref=sc_tx,
            dst_ref=sc_rx.at[k - 1],
            send_sem=sc_send.at[k - 1],
            recv_sem=sc_recv.at[k - 1],
            device_id={"tensor": (x + k) % NX},
            device_id_type=MESH,
        ).start()

    cp_gate.wait()
    cp_up.wait()
    for i in range(8):
        part = slice(i * 128, (i + 1) * 128)
        a = gate[:, part].astype(F32)
        b = up[:, part].astype(F32)
        sigma = 1.0 / (1.0 + jnp.exp(-a))
        fac_u[:, part] = a * sigma
        fac_g[:, part] = b * sigma * (1.0 + a * (1.0 - sigma))

    def place(ch, first, second):
        if ch == 0:
            return xs[first] * 4 + ys[second]
        return xs[second] * 4 + ys[first]

    def side_of(ch):
        return c if ch == 0 else 1 - c

    def push(ch, j, first, second, along_first, way, part, slot):
        if not GATHER:
            return
        axis_x = along_first == (ch == 0)
        if axis_x:
            where = {"tensor": xs[way]}
        else:
            where = {"dp": ys[way] * 2 + c}
        ref = rows.at[j, place(ch, first, second), side_of(ch)]
        if part is not None:
            ref = ref.at[pl.ds(part * 64, 64)]
        pltpu.make_async_remote_copy(
            src_ref=ref,
            dst_ref=ref,
            send_sem=a_send.at[j],
            recv_sem=a_recv.at[ch, j, slot],
            device_id=where,
            device_id_type=MESH,
        ).start()

    def arrived(ch, j, first, second, part, slot):
        if not GATHER:
            return
        ref = rows.at[j, place(ch, first, second), side_of(ch)]
        if part is not None:
            ref = ref.at[pl.ds(part * 64, 64)]
        pltpu.make_async_copy(ref, ref, a_recv.at[ch, j, slot]).wait()

    def spread(ch, j, first):
        push(ch, j, first, OWN, False, PLUS, None, 4 + 4 * first)
        push(ch, j, first, OWN, False, MINUS, None, 5 + 4 * first)

    def step_a(ch, j):
        push(ch, j, OWN, OWN, True, PLUS, None, 0)
        push(ch, j, OWN, OWN, True, MINUS, None, 1)
        spread(ch, j, OWN)

    def step_b(ch, j):
        arrived(ch, j, MINUS, OWN, None, 0)
        push(ch, j, MINUS, OWN, True, PLUS, 0, 2)
        spread(ch, j, MINUS)
        arrived(ch, j, PLUS, OWN, None, 1)
        push(ch, j, PLUS, OWN, True, MINUS, 1, 3)
        spread(ch, j, PLUS)

    def step_c(ch, j):
        arrived(ch, j, OPP, OWN, 0, 2)
        arrived(ch, j, OPP, OWN, 1, 3)
        spread(ch, j, OPP)

    def step_d(ch, j, first):
        arrived(ch, j, first, MINUS, None, 4 + 4 * first)
        push(ch, j, first, MINUS, False, PLUS, 0, 6 + 4 * first)
        arrived(ch, j, first, PLUS, None, 5 + 4 * first)
        push(ch, j, first, PLUS, False, MINUS, 1, 7 + 4 * first)

    def step_e(ch, j, first):
        arrived(ch, j, first, OPP, 0, 6 + 4 * first)
        arrived(ch, j, first, OPP, 1, 7 + 4 * first)

    out_row = lax.broadcasted_iota(jnp.int32, (256, 256), 0)
    in_row = lax.broadcasted_iota(jnp.int32, (256, 256), 1)
    src = (z + NZ - (out_row // 2) % 16) % NZ
    want = src * 16 + (out_row // 128) * 8 + ((out_row // 32) % 4) * 2 + out_row % 2
    perm = (in_row == want).astype(BF16)

    def unpack(ch, j):
        if DISPATCH:
            got = (rx_same.at[j, pl.ds(1, 15)], rx_cross.at[j])[ch]
            pltpu.make_async_copy(got, got, z_recv.at[j, ch]).wait()
        packets = (rx_same, rx_cross)[ch][j].reshape(256, 128)
        out = jnp.dot(perm, packets, preferred_element_type=F32).astype(BF16)
        for f in range(2):
            rows[j, place(ch, OWN, OWN), side_of(ch), :, f * 128 : (f + 1) * 128] = out[f * 128 : (f + 1) * 128]
        step_a(ch, j)

    def matmul(j, rel):
        if not MATMUL:
            return
        total = [None, None]
        for q in range(NX):
            block = rows[j, q * 4 + ys[rel]].reshape(2 * ROWS, PART)
            for side in (0, 1):
                term = lax.dot_general(
                    wbuf[side, q, :, j * PART : (j + 1) * PART],
                    block,
                    (((1,), (1,)), ((), ())),
                    preferred_element_type=F32,
                )
                total[side] = term if total[side] is None else total[side] + term
        if j == 0:
            p_own[rel] = total[0]
            p_tx[rel] = total[1]
            return
        p_tx[rel] = p_tx[rel] + total[1]
        pltpu.make_async_remote_copy(
            src_ref=p_tx.at[rel],
            dst_ref=p_rx.at[rel],
            send_sem=p_send.at[rel],
            recv_sem=p_recv.at[rel],
            device_id={"dp": partner},
            device_id_type=MESH,
        ).start()
        p_own[rel] = p_own[rel] + total[0]

    def finish(rel):
        if not MATMUL:
            return
        pltpu.make_async_copy(p_rx.at[rel], p_rx.at[rel], p_recv.at[rel]).wait()
        hidden = p_own[rel] + p_rx[rel]
        at = pl.ds(pl.multiple_of(ys[rel] * 256, 256), 256)
        ug_ref[0, :, at] = (hidden * fac_u[:, at]).astype(BF16)
        gg_ref[0, :, at] = (hidden * fac_g[:, at]).astype(BF16)

    def router_a():
        if not ROUTER:
            return
        for k in range(1, NX):
            pltpu.make_async_copy(sc_rx.at[k - 1], sc_rx.at[k - 1], sc_recv.at[k - 1]).wait()
        total = sc_tx[...] + sc_rx[0] + sc_rx[1] + sc_rx[2]
        diff = total[0:1, :] * keep[0] - total[1:2, :] * keep[1]
        coef = wts[0] * wts[1] * diff
        logit_grad = coef * (hot[0] - hot[1])
        high = logit_grad.astype(BF16)
        rest = logit_grad - high.astype(F32)
        mid = rest.astype(BF16)
        low = (rest - mid.astype(F32)).astype(BF16)
        cp_tok.wait()
        terms = jnp.dot(
            jnp.concatenate([high, mid, low], axis=0), tok[...], preferred_element_type=F32
        )
        term = terms[0:16] + terms[16:32] + terms[32:48]
        for p in range(16):
            rt[p] = term[(p // 8) * 8 : (p // 8) * 8 + 8, (p % 8) * 128 : (p % 8) * 128 + 128]
        for k in range(1, NZ):
            to = (z + k) % NZ
            pltpu.make_async_remote_copy(
                src_ref=rt.at[to],
                dst_ref=r1.at[k - 1],
                send_sem=r_send.at[0],
                recv_sem=r_recv.at[0],
                device_id={"expert": to},
                device_id_type=MESH,
            ).start()

    def router_b():
        if not ROUTER:
            return
        pltpu.make_async_copy(r1, r1, r_recv.at[0]).wait()
        total = rt[z]
        for k in range(NZ - 1):
            total = total + r1[k]
        r2[dp] = total
        for k in range(1, 2 * NY):
            pltpu.make_async_remote_copy(
                src_ref=r2.at[dp],
                dst_ref=r2.at[dp],
                send_sem=r_send.at[1],
                recv_sem=r_recv.at[1],
                device_id={"dp": (dp + k) % (2 * NY)},
                device_id_type=MESH,
            ).start()

    def router_c():
        if not ROUTER:
            return
        pltpu.make_async_copy(r2.at[pl.ds(0, 7)], r2.at[pl.ds(0, 7)], r_recv.at[1]).wait()
        total = r2[0]
        for k in range(1, 2 * NY):
            total = total + r2[k]
        r3[z] = total
        for k in range(1, NZ):
            pltpu.make_async_remote_copy(
                src_ref=r3.at[z],
                dst_ref=r3.at[z],
                send_sem=r_send.at[2],
                recv_sem=r_recv.at[2],
                device_id={"expert": (z + k) % NZ},
                device_id_type=MESH,
            ).start()

    def router_d():
        if not ROUTER:
            return
        pltpu.make_async_copy(r3.at[pl.ds(0, 15)], r3.at[pl.ds(0, 15)], r_recv.at[2]).wait()
        for p in range(16):
            rg_ref[(p // 8) * 8 : (p // 8) * 8 + 8, (p % 8) * 128 : (p % 8) * 128 + 128] = r3[p]

    def unpacked(t):
        unpack(t % 2, t // 2)

    def near(t):
        step_b(t % 2, t // 2)

    def across(t):
        step_c(t % 2, t // 2)

    def onward(t, first):
        step_d(t % 2, t // 2, first)

    def last(t):
        for first in range(4):
            step_e(t % 2, t // 2, first)

    unpacked(0)
    router_a()
    unpacked(1)
    near(0)
    onward(0, OWN)
    unpacked(2)
    across(0)
    near(1)
    onward(1, OWN)
    unpacked(3)
    onward(0, MINUS)
    across(1)
    near(2)
    onward(2, OWN)
    onward(0, PLUS)
    router_b()
    near(3)
    onward(1, MINUS)
    onward(3, OWN)
    across(2)
    onward(0, OPP)
    across(3)
    onward(1, PLUS)
    onward(2, MINUS)
    onward(1, OPP)
    onward(3, MINUS)
    pltpu.make_async_copy(wbuf.at[0], wbuf.at[0], w_sem.at[0]).wait()
    pltpu.make_async_copy(wbuf.at[1], wbuf.at[1], wr_sem.at[1]).wait()
    step_e(1, 0, OWN)
    matmul(0, OWN)
    router_c()
    onward(2, PLUS)
    step_e(1, 0, MINUS)
    matmul(0, MINUS)
    onward(3, PLUS)
    step_e(1, 0, PLUS)
    matmul(0, PLUS)
    onward(2, OPP)
    step_e(1, 0, OPP)
    for first in range(4):
        step_e(0, 0, first)
    matmul(0, OPP)
    onward(3, OPP)
    step_e(1, 1, OWN)
    matmul(1, OWN)
    step_e(1, 1, MINUS)
    matmul(1, MINUS)
    step_e(1, 1, PLUS)
    matmul(1, PLUS)
    router_d()
    finish(OWN)
    for first in range(4):
        step_e(0, 1, first)
    step_e(1, 1, OPP)
    matmul(1, OPP)
    finish(MINUS)
    finish(PLUS)
    if not ROUTER:
        cp_tok.wait()

    for j in range(NJ):
        if DISPATCH:
            pltpu.make_async_copy(tx.at[j, pl.ds(0, 31)], tx.at[j, pl.ds(0, 31)], z_send.at[j]).wait()
        if GATHER:
            sent = rows.at[j, pl.ds(0, 15)]
            pltpu.make_async_copy(sent, sent, a_send.at[j]).wait()
    if ROUTER:
        for k in range(NX - 1):
            pltpu.make_async_copy(sc_tx, sc_tx, sc_send.at[k]).wait()
        pltpu.make_async_copy(r1, r1, r_send.at[0]).wait()
        pltpu.make_async_copy(r2.at[pl.ds(0, 7)], r2.at[pl.ds(0, 7)], r_send.at[1]).wait()
        pltpu.make_async_copy(r1, r1, r_send.at[2]).wait()
    pltpu.make_async_copy(wbuf.at[1], wbuf.at[1], wr_sem.at[0]).wait()
    finish(OPP)
    if MATMUL:
        for rel in range(NY):
            pltpu.make_async_copy(p_tx.at[rel], p_tx.at[rel], p_send.at[rel]).wait()


def body(
    grad_out,
    tokens_in,
    router_logits,
    expert_ids,
    slot_index,
    kept,
    expert_out,
    gate_pre,
    up_pre,
    down_weight,
):
    hbm = pl.BlockSpec(memory_space=pltpu.HBM)
    vmem = pl.BlockSpec(memory_space=pltpu.VMEM)
    dma = pltpu.SemaphoreType.DMA
    slots = gate_pre.shape[1]
    gate_grad, up_grad, router_grad = pl.pallas_call(
        kernel,
        out_shape=(
            jax.ShapeDtypeStruct((1, HID, slots), BF16),
            jax.ShapeDtypeStruct((1, HID, slots), BF16),
            jax.ShapeDtypeStruct((16, 1024), F32),
        ),
        in_specs=[hbm] * 10,
        out_specs=(vmem, vmem, vmem),
        scratch_shapes=[
            pltpu.VMEM((128, 1024), BF16),
            pltpu.VMEM((128, 1024), BF16),
            pltpu.VMEM((128, 2, 1024), BF16),
            pltpu.VMEM((HID, slots), BF16),
            pltpu.VMEM((HID, slots), BF16),
            pltpu.VMEM((16, 128), F32),
            pltpu.VMEM((2, 128), jnp.int32),
            pltpu.VMEM((2, 128), jnp.int32),
            pltpu.VMEM((2, 128), jnp.int32),
            pltpu.VMEM((2, NX, HID, HALF), BF16),
            pltpu.VMEM((HID, slots), F32),
            pltpu.VMEM((HID, slots), F32),
            pltpu.VMEM((NJ, 2 * NZ, 16, 128), BF16),
            pltpu.VMEM((NJ, NZ, 16, 128), BF16),
            pltpu.VMEM((NJ, NZ, 16, 128), BF16),
            pltpu.VMEM((NJ, NX * NY, 2, ROWS, PART), BF16),
            pltpu.VMEM((NY, HID, 2 * ROWS), F32),
            pltpu.VMEM((NY, HID, 2 * ROWS), F32),
            pltpu.VMEM((NY, HID, 2 * ROWS), F32),
            pltpu.VMEM((8, 128), F32),
            pltpu.VMEM((NX - 1, 8, 128), F32),
            pltpu.VMEM((NZ, 8, 128), F32),
            pltpu.VMEM((NZ - 1, 8, 128), F32),
            pltpu.VMEM((2 * NY, 8, 128), F32),
            pltpu.VMEM((NZ, 8, 128), F32),
            dma((9,)),
            dma((1,)),
            dma((2,)),
            dma((NJ,)),
            dma((NJ, 2)),
            dma((NJ,)),
            dma((2, NJ, 20)),
            dma((NY,)),
            dma((NY,)),
            dma((NX - 1,)),
            dma((NX - 1,)),
            dma((3,)),
            dma((3,)),
        ],
        compiler_params=pltpu.CompilerParams(
            collective_id=0, has_side_effects=True, vmem_limit_bytes=24 * 1024 * 1024
        ),
    )(
        *(
            pltpu.with_memory_space_constraint(arg, pltpu.HBM)
            for arg in (
                grad_out,
                tokens_in,
                expert_out,
                jnp.swapaxes(gate_pre, 1, 2),
                jnp.swapaxes(up_pre, 1, 2),
                down_weight,
                router_logits.T,
                expert_ids.T,
                slot_index.T,
                kept.T,
            )
        )
    )
    return jnp.swapaxes(gate_grad, 1, 2), jnp.swapaxes(up_grad, 1, 2), router_grad


def solution(mesh):
    in_specs = (
        P(("dp", "expert"), "tensor"),
        P(("dp", "expert"), "tensor"),
        P(("dp", "expert"), None),
        P(("dp", "expert"), None),
        P(("dp", "expert"), None),
        P(("dp", "expert"), None),
        P(("dp", "expert"), None, "tensor"),
        P("expert", None, ("dp", "tensor")),
        P("expert", None, ("dp", "tensor")),
        P("expert", ("dp", "tensor"), None),
    )
    out_specs = (
        P("expert", None, ("dp", "tensor")),
        P("expert", None, ("dp", "tensor")),
        P(None, "tensor"),
    )
    return jax.shard_map(body, mesh=mesh, in_specs=in_specs, out_specs=out_specs, check_vma=False)
```

```python
import functools

import jax
import jax.numpy as jnp
from jax import lax
from jax.experimental import pallas as pl
from jax.experimental.pallas import tpu as pltpu
from jax.sharding import PartitionSpec as P

MESH = pl.DeviceIdType.MESH
F32 = jnp.float32
BF16 = jnp.bfloat16

NZ = 16
NX = 4
NY = 4
NJ = 2
HID = 224
HALF = 512
ROWS = 128
PART = HALF // NJ

OWN, MINUS, PLUS, OPP = 0, 1, 2, 3


def kernel(
    g_hbm, tok_hbm, eo_hbm, gate_hbm, up_hbm, w_hbm, logits_hbm, ids_hbm, slot_hbm, kept_hbm,
    gg_ref, ug_ref, rg_ref,
    g, tok, eo, gate, up, logits_ref, ids_ref, slot_ref, kept_ref, wbuf, fac_u, fac_g,
    tx, rx_same, rx_cross, rows, p_own, p_tx, p_rx,
    sc_tx, sc_rx, rt, r1, r2, r3,
    in_sem, w_sem, wr_sem, z_send, z_recv, a_send, a_recv, p_send, p_recv,
    sc_send, sc_recv, r_send, r_recv,
):
    dp = lax.axis_index("dp")
    z = lax.axis_index("expert")
    x = lax.axis_index("tensor")
    y = dp // 2
    c = dp % 2
    partner = dp + 1 - 2 * c
    xs = [x, (x + 3) % 4, (x + 1) % 4, (x + 2) % 4]
    ys = [y, (y + 3) % 4, (y + 1) % 4, (y + 2) % 4]

    def fetch(i, src, dst):
        copy = pltpu.make_async_copy(src, dst, in_sem.at[i])
        copy.start()
        return copy

    routes = [
        fetch(5, logits_hbm, logits_ref),
        fetch(6, ids_hbm, ids_ref),
        fetch(7, slot_hbm, slot_ref),
        fetch(8, kept_hbm, kept_ref),
    ]
    cp_g = fetch(0, g_hbm, g)

    barrier = pltpu.get_barrier_semaphore()

    def greet(**where):
        pl.semaphore_signal(barrier, inc=1, device_id=where, device_id_type=MESH)

    far_first = [NZ // 2]
    for k in range(NZ // 2 - 1, 0, -1):
        far_first += [k, NZ - k]
    for k in far_first:
        greet(expert=(z + k) % NZ)
        greet(expert=(z + k) % NZ, dp=partner)
    for k in range(1, NX):
        greet(tensor=(x + k) % NX)
    for k in range(1, 2 * NY):
        greet(dp=(dp + k) % (2 * NY))

    for copy in routes:
        copy.wait()
    ids = ids_ref[...]
    slots = slot_ref[...]
    kept = kept_ref[...]
    logits = logits_ref[...]
    expert_row = lax.broadcasted_iota(jnp.int32, (16, 128), 0)
    hot = [(expert_row == ids[k : k + 1, :]).astype(F32) for k in range(2)]
    chosen = [jnp.sum(hot[k] * logits, axis=0, keepdims=True) for k in range(2)]
    w0 = 1.0 / (1.0 + jnp.exp(chosen[1] - chosen[0]))
    wts = [w0, 1.0 - w0]
    keep = [kept[k : k + 1, :].astype(F32) for k in range(2)]

    row = lax.broadcasted_iota(jnp.int32, (256, 128), 0)
    row_key = (row // 16) * 8 + row % 8
    row_blk = (row // 8) % 2
    one = jnp.zeros((256, 128), F32)
    val = jnp.zeros((256, 128), F32)
    for k in range(2):
        key = jnp.where(kept[k : k + 1, :] == 1, ids[k : k + 1, :] * 8 + slots[k : k + 1, :], -1)
        hit = (row_key == key).astype(F32)
        one = one + hit
        val = val + hit * wts[k]
    scale = jnp.sum(val, axis=1, keepdims=True)
    wide = jnp.concatenate(
        [jnp.where(row_blk == f, one, 0.0).astype(BF16) for f in range(2)], axis=1
    )
    cp_g.wait()

    def pack(j):
        for h in range(2):
            at = h * HALF + j * PART
            tall = jnp.concatenate([g[:, at : at + 128], g[:, at + 128 : at + 256]], axis=0)
            picked = jnp.dot(wide, tall, preferred_element_type=F32)
            tx[j, h * NZ : (h + 1) * NZ] = (picked * scale).astype(BF16).reshape(NZ, 16, 128)

    pack(0)
    pl.semaphore_wait(barrier, 2 * (NZ - 1) + (NX - 1) + (2 * NY - 1))

    for j in range(NJ):
        if j > 0:
            pack(j)
        rx_same[j, 0] = tx[j, c * NZ + z]
        for k in far_first:
            to = (z + k) % NZ
            pltpu.make_async_remote_copy(
                src_ref=tx.at[j, c * NZ + to],
                dst_ref=rx_same.at[j, k],
                send_sem=z_send.at[j],
                recv_sem=z_recv.at[j, 0],
                device_id={"expert": to},
                device_id_type=MESH,
            ).start()
        for k in far_first + [0]:
            to = (z + k) % NZ
            pltpu.make_async_remote_copy(
                src_ref=tx.at[j, (1 - c) * NZ + to],
                dst_ref=rx_cross.at[j, k],
                send_sem=z_send.at[j],
                recv_sem=z_recv.at[j, 1],
                device_id={"expert": to, "dp": partner},
                device_id_type=MESH,
            ).start()

    cp_eo = fetch(1, eo_hbm, eo)
    cp_tok = fetch(2, tok_hbm, tok)
    cp_gate = fetch(3, gate_hbm.at[0], gate)
    cp_up = fetch(4, up_hbm.at[0], up)

    def weight(core, q, j):
        return w_hbm.at[0, :, pl.ds(pl.multiple_of(q * 1024 + core * HALF + j * PART, PART), PART)]

    for j in range(NJ):
        for q in range(NX):
            pltpu.make_async_copy(
                weight(c, q, j), wbuf.at[j, pl.ds(0, HID), pl.ds(q * PART, PART)], w_sem.at[j]
            ).start()

    for j in range(NJ):
        for q in range(NX):
            pltpu.make_async_remote_copy(
                src_ref=weight(1 - c, q, j),
                dst_ref=wbuf.at[j, pl.ds(HID, HID), pl.ds(q * PART, PART)],
                send_sem=wr_sem.at[0, j],
                recv_sem=wr_sem.at[1, j],
                device_id={"dp": partner},
                device_id_type=MESH,
            ).start()

    cp_eo.wait()
    parts = [jnp.zeros((128, 128), F32) for _ in range(2)]
    for f in range(8):
        cols = slice(f * 128, (f + 1) * 128)
        grad = g[:, cols].astype(F32)
        both = eo[:, :, cols].astype(F32)
        for k in range(2):
            parts[k] = parts[k] + grad * both[:, k, :]
    score = [jnp.sum(parts[k].T, axis=0, keepdims=True) for k in range(2)]
    sub = lax.broadcasted_iota(jnp.int32, (8, 128), 0)
    sc_tx[...] = jnp.where(sub == 0, score[0], jnp.where(sub == 1, score[1], 0.0))
    for k in range(1, NX):
        pltpu.make_async_remote_copy(
            src_ref=sc_tx,
            dst_ref=sc_rx.at[k - 1],
            send_sem=sc_send.at[k - 1],
            recv_sem=sc_recv.at[k - 1],
            device_id={"tensor": (x + k) % NX},
            device_id_type=MESH,
        ).start()

    cp_gate.wait()
    cp_up.wait()
    for i in range(8):
        part = slice(i * 128, (i + 1) * 128)
        a = gate[:, part].astype(F32)
        b = up[:, part].astype(F32)
        sigma = 1.0 / (1.0 + jnp.exp(-a))
        fac_u[:, part] = a * sigma
        fac_g[:, part] = b * sigma * (1.0 + a * (1.0 - sigma))

    def place(o, first, second):
        if o == 0:
            return ys[second] * NX + xs[first]
        return ys[first] * NX + xs[second]

    def block(o, ch, j, first, second, half):
        core = c if ch == 0 else 1 - c
        some = pl.ds(0, 128) if half is None else pl.ds(half * 64, 64)
        return rows.at[
            j, place(o, first, second), o, some, pl.ds(pl.multiple_of(core * 128, 128), 128)
        ]

    def push(o, ch, j, first, second, along_first, way, half, slot):
        if along_first == (o == 0):
            where = {"tensor": xs[way]}
        else:
            where = {"dp": ys[way] * 2 + c}
        ref = block(o, ch, j, first, second, half)
        pltpu.make_async_remote_copy(
            src_ref=ref,
            dst_ref=ref,
            send_sem=a_send.at[j],
            recv_sem=a_recv.at[o, ch, j, slot],
            device_id=where,
            device_id_type=MESH,
        ).start()

    def arrived(o, ch, j, first, second, half, slot):
        ref = block(o, ch, j, first, second, half)
        pltpu.make_async_copy(ref, ref, a_recv.at[o, ch, j, slot]).wait()

    def spread(o, ch, j, first):
        push(o, ch, j, first, OWN, False, PLUS, None, 4 + 4 * first)
        push(o, ch, j, first, OWN, False, MINUS, None, 5 + 4 * first)

    def step_a(o, ch, j):
        push(o, ch, j, OWN, OWN, True, PLUS, None, 0)
        push(o, ch, j, OWN, OWN, True, MINUS, None, 1)

    def step_b(o, ch, j):
        arrived(o, ch, j, MINUS, OWN, None, 0)
        push(o, ch, j, MINUS, OWN, True, PLUS, 0, 2)
        arrived(o, ch, j, PLUS, OWN, None, 1)
        push(o, ch, j, PLUS, OWN, True, MINUS, 1, 3)

    def step_c(o, ch, j):
        arrived(o, ch, j, OPP, OWN, 0, 2)
        arrived(o, ch, j, OPP, OWN, 1, 3)
        spread(o, ch, j, OPP)

    def step_d(o, ch, j, first):
        arrived(o, ch, j, first, MINUS, None, 4 + 4 * first)
        push(o, ch, j, first, MINUS, False, PLUS, 0, 6 + 4 * first)
        arrived(o, ch, j, first, PLUS, None, 5 + 4 * first)
        push(o, ch, j, first, PLUS, False, MINUS, 1, 7 + 4 * first)

    def step_e(o, ch, j, first):
        arrived(o, ch, j, first, OPP, 0, 6 + 4 * first)
        arrived(o, ch, j, first, OPP, 1, 7 + 4 * first)

    out_row = lax.broadcasted_iota(jnp.int32, (256, 256), 0)
    in_row = lax.broadcasted_iota(jnp.int32, (256, 256), 1)
    src = (z + NZ - (out_row // 2) % 16) % NZ
    want = src * 16 + (out_row // 128) * 8 + ((out_row // 32) % 4) * 2 + out_row % 2
    perm = (in_row == want).astype(BF16)

    def unpacked(t):
        ch, j = t % 2, t // 2
        got = (rx_same.at[j, pl.ds(1, 15)], rx_cross.at[j])[ch]
        pltpu.make_async_copy(got, got, z_recv.at[j, ch]).wait()
        packets = (rx_same, rx_cross)[ch][j].reshape(256, 128)
        out = jnp.dot(perm, packets, preferred_element_type=F32)
        for o in range(2):
            ref = block(o, ch, j, OWN, OWN, None)
            ref[...] = out[o * 128 : (o + 1) * 128].T.astype(BF16)
            step_a(o, ch, j)
        for o in range(2):
            spread(o, ch, j, OWN)

    def near(t):
        for o in range(2):
            step_b(o, t % 2, t // 2)
        for o in range(2):
            spread(o, t % 2, t // 2, MINUS)
            spread(o, t % 2, t // 2, PLUS)

    def across(t):
        for o in range(2):
            step_c(o, t % 2, t // 2)

    def onward(t, first):
        for o in range(2):
            step_d(o, t % 2, t // 2, first)

    def matmul(j, rel):
        for ch in range(2):
            step_e(1, ch, j, rel)
            if rel == OPP:
                for first in range(4):
                    step_e(0, ch, j, first)
        cols = rows[j, pl.ds(ys[rel] * NX, NX)].reshape(NX * PART, 2 * ROWS)
        total = jnp.dot(wbuf[j], cols, preferred_element_type=F32)
        if j == 0:
            p_own[rel] = total[0:HID]
            p_tx[rel] = total[HID : 2 * HID]
            return
        p_tx[rel] = p_tx[rel] + total[HID : 2 * HID]
        pltpu.make_async_remote_copy(
            src_ref=p_tx.at[rel],
            dst_ref=p_rx.at[rel],
            send_sem=p_send.at[rel],
            recv_sem=p_recv.at[rel],
            device_id={"dp": partner},
            device_id_type=MESH,
        ).start()
        p_own[rel] = p_own[rel] + total[0:HID]

    def finish(rel):
        pltpu.make_async_copy(p_rx.at[rel], p_rx.at[rel], p_recv.at[rel]).wait()
        hidden = p_own[rel] + p_rx[rel]
        at = pl.ds(pl.multiple_of(ys[rel] * 256, 256), 256)
        ug_ref[0, :, at] = (hidden * fac_u[:, at]).astype(BF16)
        gg_ref[0, :, at] = (hidden * fac_g[:, at]).astype(BF16)

    def router_a():
        for k in range(1, NX):
            pltpu.make_async_copy(sc_rx.at[k - 1], sc_rx.at[k - 1], sc_recv.at[k - 1]).wait()
        total = sc_tx[...] + sc_rx[0] + sc_rx[1] + sc_rx[2]
        diff = total[0:1, :] * keep[0] - total[1:2, :] * keep[1]
        coef = wts[0] * wts[1] * diff
        logit_grad = coef * (hot[0] - hot[1])
        high = logit_grad.astype(BF16)
        rest = logit_grad - high.astype(F32)
        mid = rest.astype(BF16)
        low = (rest - mid.astype(F32)).astype(BF16)
        cp_tok.wait()
        terms = jnp.dot(
            jnp.concatenate([high, mid, low], axis=0), tok[...], preferred_element_type=F32
        )
        term = terms[0:16] + terms[16:32] + terms[32:48]
        for p in range(16):
            rt[p] = term[(p // 8) * 8 : (p // 8) * 8 + 8, (p % 8) * 128 : (p % 8) * 128 + 128]

    def router_e():
        for k in range(1, NZ):
            to = (z + k) % NZ
            pltpu.make_async_remote_copy(
                src_ref=rt.at[to],
                dst_ref=r1.at[k - 1],
                send_sem=r_send.at[0],
                recv_sem=r_recv.at[0],
                device_id={"expert": to},
                device_id_type=MESH,
            ).start()

    def router_b():
        pltpu.make_async_copy(r1, r1, r_recv.at[0]).wait()
        total = rt[z]
        for k in range(NZ - 1):
            total = total + r1[k]
        r2[dp] = total
        for k in range(1, 2 * NY):
            pltpu.make_async_remote_copy(
                src_ref=r2.at[dp],
                dst_ref=r2.at[dp],
                send_sem=r_send.at[1],
                recv_sem=r_recv.at[1],
                device_id={"dp": (dp + k) % (2 * NY)},
                device_id_type=MESH,
            ).start()

    def router_c():
        pltpu.make_async_copy(r2.at[pl.ds(0, 7)], r2.at[pl.ds(0, 7)], r_recv.at[1]).wait()
        total = r2[0]
        for k in range(1, 2 * NY):
            total = total + r2[k]
        r3[z] = total
        for k in range(1, NZ):
            pltpu.make_async_remote_copy(
                src_ref=r3.at[z],
                dst_ref=r3.at[z],
                send_sem=r_send.at[2],
                recv_sem=r_recv.at[2],
                device_id={"expert": (z + k) % NZ},
                device_id_type=MESH,
            ).start()

    def router_d():
        pltpu.make_async_copy(r3.at[pl.ds(0, 15)], r3.at[pl.ds(0, 15)], r_recv.at[2]).wait()
        for p in range(16):
            rg_ref[(p // 8) * 8 : (p // 8) * 8 + 8, (p % 8) * 128 : (p % 8) * 128 + 128] = r3[p]

    def weights_here():
        for j in range(NJ):
            own, other = wbuf.at[j, pl.ds(0, HID)], wbuf.at[j, pl.ds(HID, HID)]
            pltpu.make_async_copy(own, own, w_sem.at[j]).wait()
            pltpu.make_async_copy(other, other, wr_sem.at[1, j]).wait()

    router_a()
    router_e()
    unpacked(0)
    unpacked(1)
    near(0)
    onward(0, OWN)
    unpacked(2)
    near(1)
    onward(1, OWN)
    across(0)
    onward(0, MINUS)
    onward(0, PLUS)
    unpacked(3)
    near(2)
    onward(2, OWN)
    across(1)
    onward(1, MINUS)
    onward(1, PLUS)
    router_b()
    near(3)
    onward(3, OWN)
    across(2)
    onward(2, MINUS)
    onward(2, PLUS)
    onward(0, OPP)
    onward(1, OPP)
    across(3)
    onward(3, MINUS)
    onward(3, PLUS)
    router_c()
    weights_here()
    matmul(0, OWN)
    matmul(0, MINUS)
    onward(2, OPP)
    matmul(0, PLUS)
    matmul(0, OPP)
    onward(3, OPP)
    matmul(1, OWN)
    matmul(1, MINUS)
    matmul(1, PLUS)
    finish(OWN)
    matmul(1, OPP)
    finish(MINUS)
    finish(PLUS)
    router_d()
    for j in range(NJ):
        pltpu.make_async_copy(tx.at[j, pl.ds(0, 31)], tx.at[j, pl.ds(0, 31)], z_send.at[j]).wait()
        sent = rows.at[j, pl.ds(0, 15)]
        pltpu.make_async_copy(sent, sent, a_send.at[j]).wait()
    for k in range(NX - 1):
        pltpu.make_async_copy(sc_tx, sc_tx, sc_send.at[k]).wait()
    pltpu.make_async_copy(r1, r1, r_send.at[0]).wait()
    pltpu.make_async_copy(r2.at[pl.ds(0, 7)], r2.at[pl.ds(0, 7)], r_send.at[1]).wait()
    pltpu.make_async_copy(r1, r1, r_send.at[2]).wait()
    for j in range(NJ):
        other = wbuf.at[j, pl.ds(HID, HID)]
        pltpu.make_async_copy(other, other, wr_sem.at[0, j]).wait()
    finish(OPP)
    for rel in range(NY):
        pltpu.make_async_copy(p_tx.at[rel], p_tx.at[rel], p_send.at[rel]).wait()


def body(
    grad_out,
    tokens_in,
    router_logits,
    expert_ids,
    slot_index,
    kept,
    expert_out,
    gate_pre,
    up_pre,
    down_weight,
):
    hbm = pl.BlockSpec(memory_space=pltpu.HBM)
    vmem = pl.BlockSpec(memory_space=pltpu.VMEM)
    dma = pltpu.SemaphoreType.DMA
    slots = gate_pre.shape[1]
    gate_grad, up_grad, router_grad = pl.pallas_call(
        kernel,
        out_shape=(
            jax.ShapeDtypeStruct((1, HID, slots), BF16),
            jax.ShapeDtypeStruct((1, HID, slots), BF16),
            jax.ShapeDtypeStruct((16, 1024), F32),
        ),
        in_specs=[hbm] * 10,
        out_specs=(vmem, vmem, vmem),
        scratch_shapes=[
            pltpu.VMEM((128, 1024), BF16),
            pltpu.VMEM((128, 1024), BF16),
            pltpu.VMEM((128, 2, 1024), BF16),
            pltpu.VMEM((HID, slots), BF16),
            pltpu.VMEM((HID, slots), BF16),
            pltpu.VMEM((16, 128), F32),
            pltpu.VMEM((2, 128), jnp.int32),
            pltpu.VMEM((2, 128), jnp.int32),
            pltpu.VMEM((2, 128), jnp.int32),
            pltpu.VMEM((NJ, 2 * HID, NX * PART), BF16),
            pltpu.VMEM((HID, slots), F32),
            pltpu.VMEM((HID, slots), F32),
            pltpu.VMEM((NJ, 2 * NZ, 16, 128), BF16),
            pltpu.VMEM((NJ, NZ, 16, 128), BF16),
            pltpu.VMEM((NJ, NZ, 16, 128), BF16),
            pltpu.VMEM((NJ, NY * NX, 2, PART // 2, 2 * ROWS), BF16),
            pltpu.VMEM((NY, HID, 2 * ROWS), F32),
            pltpu.VMEM((NY, HID, 2 * ROWS), F32),
            pltpu.VMEM((NY, HID, 2 * ROWS), F32),
            pltpu.VMEM((8, 128), F32),
            pltpu.VMEM((NX - 1, 8, 128), F32),
            pltpu.VMEM((NZ, 8, 128), F32),
            pltpu.VMEM((NZ - 1, 8, 128), F32),
            pltpu.VMEM((2 * NY, 8, 128), F32),
            pltpu.VMEM((NZ, 8, 128), F32),
            dma((9,)),
            dma((NJ,)),
            dma((2, NJ)),
            dma((NJ,)),
            dma((NJ, 2)),
            dma((NJ,)),
            dma((2, 2, NJ, 20)),
            dma((NY,)),
            dma((NY,)),
            dma((NX - 1,)),
            dma((NX - 1,)),
            dma((3,)),
            dma((3,)),
        ],
        compiler_params=pltpu.CompilerParams(
            collective_id=0, has_side_effects=True, vmem_limit_bytes=24 * 1024 * 1024
        ),
    )(
        *(
            pltpu.with_memory_space_constraint(arg, pltpu.HBM)
            for arg in (
                grad_out,
                tokens_in,
                expert_out,
                jnp.swapaxes(gate_pre, 1, 2),
                jnp.swapaxes(up_pre, 1, 2),
                down_weight,
                router_logits.T,
                expert_ids.T,
                slot_index.T,
                kept.T,
            )
        )
    )
    return jnp.swapaxes(gate_grad, 1, 2), jnp.swapaxes(up_grad, 1, 2), router_grad


def solution(mesh):
    in_specs = (
        P(("dp", "expert"), "tensor"),
        P(("dp", "expert"), "tensor"),
        P(("dp", "expert"), None),
        P(("dp", "expert"), None),
        P(("dp", "expert"), None),
        P(("dp", "expert"), None),
        P(("dp", "expert"), None, "tensor"),
        P("expert", None, ("dp", "tensor")),
        P("expert", None, ("dp", "tensor")),
        P("expert", ("dp", "tensor"), None),
    )
    out_specs = (
        P("expert", None, ("dp", "tensor")),
        P("expert", None, ("dp", "tensor")),
        P(None, "tensor"),
    )
    return jax.shard_map(body, mesh=mesh, in_specs=in_specs, out_specs=out_specs, check_vma=False)
```

```python
import functools

import jax
import jax.numpy as jnp
from jax import lax
from jax.experimental import pallas as pl
from jax.experimental.pallas import tpu as pltpu
from jax.sharding import PartitionSpec as P

MESH = pl.DeviceIdType.MESH
F32 = jnp.float32
BF16 = jnp.bfloat16

NZ = 16
NX = 4
NY = 4
NJ = 2
HID = 224
HALF = 512
ROWS = 128
PART = HALF // NJ

OWN, MINUS, PLUS, OPP = 0, 1, 2, 3


def kernel(
    g_hbm, tok_hbm, eo_hbm, gate_hbm, up_hbm, w_hbm, logits_hbm, ids_hbm, slot_hbm, kept_hbm,
    gg_ref, ug_ref, rg_ref,
    g, tok, eo, gate, up, logits_ref, ids_ref, slot_ref, kept_ref, wbuf, fac_u, fac_g,
    tx, rx_same, rx_cross, rows, p_own, p_tx, p_rx,
    sc_tx, sc_rx, rt, r1, r2, r3,
    in_sem, w_sem, wr_sem, z_send, z_recv, a_send, a_recv, p_send, p_recv,
    sc_send, sc_recv, r_send, r_recv,
):
    dp = lax.axis_index("dp")
    z = lax.axis_index("expert")
    x = lax.axis_index("tensor")
    y = dp // 2
    c = dp % 2
    partner = dp + 1 - 2 * c
    xs = [x, (x + 3) % 4, (x + 1) % 4, (x + 2) % 4]
    ys = [y, (y + 3) % 4, (y + 1) % 4, (y + 2) % 4]

    def fetch(i, src, dst):
        copy = pltpu.make_async_copy(src, dst, in_sem.at[i])
        copy.start()
        return copy

    routes = [
        fetch(5, logits_hbm, logits_ref),
        fetch(6, ids_hbm, ids_ref),
        fetch(7, slot_hbm, slot_ref),
        fetch(8, kept_hbm, kept_ref),
    ]
    cp_g = fetch(0, g_hbm, g)

    barrier = pltpu.get_barrier_semaphore()

    def greet(**where):
        pl.semaphore_signal(barrier, inc=1, device_id=where, device_id_type=MESH)

    far_first = [NZ // 2]
    for k in range(NZ // 2 - 1, 0, -1):
        far_first += [k, NZ - k]
    for k in far_first:
        greet(expert=(z + k) % NZ)
        greet(expert=(z + k) % NZ, dp=partner)
    for k in range(1, NX):
        greet(tensor=(x + k) % NX)
    for k in range(1, 2 * NY):
        greet(dp=(dp + k) % (2 * NY))

    for copy in routes:
        copy.wait()
    ids = ids_ref[...]
    slots = slot_ref[...]
    kept = kept_ref[...]
    logits = logits_ref[...]
    expert_row = lax.broadcasted_iota(jnp.int32, (16, 128), 0)
    hot = [(expert_row == ids[k : k + 1, :]).astype(F32) for k in range(2)]
    chosen = [jnp.sum(hot[k] * logits, axis=0, keepdims=True) for k in range(2)]
    w0 = 1.0 / (1.0 + jnp.exp(chosen[1] - chosen[0]))
    wts = [w0, 1.0 - w0]
    keep = [kept[k : k + 1, :].astype(F32) for k in range(2)]

    row = lax.broadcasted_iota(jnp.int32, (256, 128), 0)
    row_key = (row // 16) * 8 + row % 8
    row_blk = (row // 8) % 2
    one = jnp.zeros((256, 128), F32)
    val = jnp.zeros((256, 128), F32)
    for k in range(2):
        key = jnp.where(kept[k : k + 1, :] == 1, ids[k : k + 1, :] * 8 + slots[k : k + 1, :], -1)
        hit = (row_key == key).astype(F32)
        one = one + hit
        val = val + hit * wts[k]
    scale = jnp.sum(val, axis=1, keepdims=True)
    wide = jnp.concatenate(
        [jnp.where(row_blk == f, one, 0.0).astype(BF16) for f in range(2)], axis=1
    )
    cp_g.wait()

    def pack(j):
        for h in range(2):
            at = h * HALF + j * PART
            tall = jnp.concatenate([g[:, at : at + 128], g[:, at + 128 : at + 256]], axis=0)
            picked = jnp.dot(wide, tall, preferred_element_type=F32)
            tx[j, h * NZ : (h + 1) * NZ] = (picked * scale).astype(BF16).reshape(NZ, 16, 128)

    pack(0)
    pl.semaphore_wait(barrier, 2 * (NZ - 1) + (NX - 1) + (2 * NY - 1))

    for j in range(NJ):
        if j > 0:
            pack(j)
        rx_same[j, 0] = tx[j, c * NZ + z]
        for k in far_first:
            to = (z + k) % NZ
            pltpu.make_async_remote_copy(
                src_ref=tx.at[j, c * NZ + to],
                dst_ref=rx_same.at[j, k],
                send_sem=z_send.at[j],
                recv_sem=z_recv.at[j, 0],
                device_id={"expert": to},
                device_id_type=MESH,
            ).start()
        for k in far_first + [0]:
            to = (z + k) % NZ
            pltpu.make_async_remote_copy(
                src_ref=tx.at[j, (1 - c) * NZ + to],
                dst_ref=rx_cross.at[j, k],
                send_sem=z_send.at[j],
                recv_sem=z_recv.at[j, 1],
                device_id={"expert": to, "dp": partner},
                device_id_type=MESH,
            ).start()

    cp_eo = fetch(1, eo_hbm, eo)
    cp_tok = fetch(2, tok_hbm, tok)
    cp_gate = fetch(3, gate_hbm.at[0], gate)
    cp_up = fetch(4, up_hbm.at[0], up)

    def weight(core, q, j):
        return w_hbm.at[0, :, pl.ds(pl.multiple_of(q * 1024 + core * HALF + j * PART, PART), PART)]

    for j in range(NJ):
        for q in range(NX):
            pltpu.make_async_copy(
                weight(c, q, j), wbuf.at[j, pl.ds(0, HID), pl.ds(q * PART, PART)], w_sem.at[j]
            ).start()

    for j in range(NJ):
        for q in range(NX):
            pltpu.make_async_remote_copy(
                src_ref=weight(1 - c, q, j),
                dst_ref=wbuf.at[j, pl.ds(HID, HID), pl.ds(q * PART, PART)],
                send_sem=wr_sem.at[0, j],
                recv_sem=wr_sem.at[1, j],
                device_id={"dp": partner},
                device_id_type=MESH,
            ).start()

    cp_eo.wait()
    parts = [jnp.zeros((128, 128), F32) for _ in range(2)]
    for f in range(8):
        cols = slice(f * 128, (f + 1) * 128)
        grad = g[:, cols].astype(F32)
        both = eo[:, :, cols].astype(F32)
        for k in range(2):
            parts[k] = parts[k] + grad * both[:, k, :]
    score = [jnp.sum(parts[k].T, axis=0, keepdims=True) for k in range(2)]
    sub = lax.broadcasted_iota(jnp.int32, (8, 128), 0)
    sc_tx[...] = jnp.where(sub == 0, score[0], jnp.where(sub == 1, score[1], 0.0))
    for k in range(1, NX):
        pltpu.make_async_remote_copy(
            src_ref=sc_tx,
            dst_ref=sc_rx.at[k - 1],
            send_sem=sc_send.at[k - 1],
            recv_sem=sc_recv.at[k - 1],
            device_id={"tensor": (x + k) % NX},
            device_id_type=MESH,
        ).start()

    cp_gate.wait()
    cp_up.wait()
    for i in range(8):
        part = slice(i * 128, (i + 1) * 128)
        a = gate[:, part].astype(F32)
        b = up[:, part].astype(F32)
        sigma = 1.0 / (1.0 + jnp.exp(-a))
        fac_u[:, part] = a * sigma
        fac_g[:, part] = b * sigma * (1.0 + a * (1.0 - sigma))

    def place(o, first, second):
        if o == 0:
            return ys[second] * NX + xs[first]
        return ys[first] * NX + xs[second]

    def block(o, ch, j, first, second, half):
        core = c if ch == 0 else 1 - c
        some = pl.ds(0, 128) if half is None else pl.ds(half * 64, 64)
        return rows.at[
            j, place(o, first, second), o, some, pl.ds(pl.multiple_of(core * 128, 128), 128)
        ]

    def push(o, ch, j, first, second, along_first, way, half, slot):
        if along_first == (o == 0):
            where = {"tensor": xs[way]}
        else:
            where = {"dp": ys[way] * 2 + c}
        ref = block(o, ch, j, first, second, half)
        pltpu.make_async_remote_copy(
            src_ref=ref,
            dst_ref=ref,
            send_sem=a_send.at[j],
            recv_sem=a_recv.at[o, ch, j, slot],
            device_id=where,
            device_id_type=MESH,
        ).start()

    def arrived(o, ch, j, first, second, half, slot):
        ref = block(o, ch, j, first, second, half)
        pltpu.make_async_copy(ref, ref, a_recv.at[o, ch, j, slot]).wait()

    def spread(o, ch, j, first):
        push(o, ch, j, first, OWN, False, PLUS, None, 4 + 4 * first)
        push(o, ch, j, first, OWN, False, MINUS, None, 5 + 4 * first)

    def step_a(o, ch, j):
        push(o, ch, j, OWN, OWN, True, PLUS, None, 0)
        push(o, ch, j, OWN, OWN, True, MINUS, None, 1)

    def step_b(o, ch, j):
        arrived(o, ch, j, MINUS, OWN, None, 0)
        push(o, ch, j, MINUS, OWN, True, PLUS, 0, 2)
        arrived(o, ch, j, PLUS, OWN, None, 1)
        push(o, ch, j, PLUS, OWN, True, MINUS, 1, 3)

    def step_c(o, ch, j):
        arrived(o, ch, j, OPP, OWN, 0, 2)
        arrived(o, ch, j, OPP, OWN, 1, 3)
        spread(o, ch, j, OPP)

    def step_d(o, ch, j, first):
        arrived(o, ch, j, first, MINUS, None, 4 + 4 * first)
        push(o, ch, j, first, MINUS, False, PLUS, 0, 6 + 4 * first)
        arrived(o, ch, j, first, PLUS, None, 5 + 4 * first)
        push(o, ch, j, first, PLUS, False, MINUS, 1, 7 + 4 * first)

    def step_e(o, ch, j, first):
        arrived(o, ch, j, first, OPP, 0, 6 + 4 * first)
        arrived(o, ch, j, first, OPP, 1, 7 + 4 * first)

    out_row = lax.broadcasted_iota(jnp.int32, (256, 256), 0)
    in_row = lax.broadcasted_iota(jnp.int32, (256, 256), 1)
    src = (z + NZ - (out_row // 2) % 16) % NZ
    want = src * 16 + (out_row // 128) * 8 + ((out_row // 32) % 4) * 2 + out_row % 2
    perm = (in_row == want).astype(BF16)

    def unpacked(t):
        ch, j = t % 2, t // 2
        got = (rx_same.at[j, pl.ds(1, 15)], rx_cross.at[j])[ch]
        pltpu.make_async_copy(got, got, z_recv.at[j, ch]).wait()
        packets = (rx_same, rx_cross)[ch][j].reshape(256, 128)
        out = jnp.dot(perm, packets, preferred_element_type=F32)
        for o in range(2):
            ref = block(o, ch, j, OWN, OWN, None)
            ref[...] = out[o * 128 : (o + 1) * 128].T.astype(BF16)
            step_a(o, ch, j)
        for o in range(2):
            spread(o, ch, j, OWN)

    def near(t):
        for o in range(2):
            step_b(o, t % 2, t // 2)
        for o in range(2):
            spread(o, t % 2, t // 2, MINUS)
            spread(o, t % 2, t // 2, PLUS)

    def across(t):
        for o in range(2):
            step_c(o, t % 2, t // 2)

    def onward(t, first):
        for o in range(2):
            step_d(o, t % 2, t // 2, first)

    def matmul(j, rel):
        for ch in range(2):
            step_e(1, ch, j, rel)
            if rel == OPP:
                for first in range(4):
                    step_e(0, ch, j, first)
        cols = rows[j, pl.ds(ys[rel] * NX, NX)].reshape(NX * PART, 2 * ROWS)
        total = jnp.dot(wbuf[j], cols, preferred_element_type=F32)
        if j == 0:
            p_own[rel] = total[0:HID]
            p_tx[rel] = total[HID : 2 * HID]
            return
        p_tx[rel] = p_tx[rel] + total[HID : 2 * HID]
        pltpu.make_async_remote_copy(
            src_ref=p_tx.at[rel],
            dst_ref=p_rx.at[rel],
            send_sem=p_send.at[rel],
            recv_sem=p_recv.at[rel],
            device_id={"dp": partner},
            device_id_type=MESH,
        ).start()
        p_own[rel] = p_own[rel] + total[0:HID]

    def finish(rel):
        pltpu.make_async_copy(p_rx.at[rel], p_rx.at[rel], p_recv.at[rel]).wait()
        hidden = p_own[rel] + p_rx[rel]
        at = pl.ds(pl.multiple_of(ys[rel] * 256, 256), 256)
        ug_ref[0, :, at] = (hidden * fac_u[:, at]).astype(BF16)
        gg_ref[0, :, at] = (hidden * fac_g[:, at]).astype(BF16)

    def router_a():
        for k in range(1, NX):
            pltpu.make_async_copy(sc_rx.at[k - 1], sc_rx.at[k - 1], sc_recv.at[k - 1]).wait()
        total = sc_tx[...] + sc_rx[0] + sc_rx[1] + sc_rx[2]
        diff = total[0:1, :] * keep[0] - total[1:2, :] * keep[1]
        coef = wts[0] * wts[1] * diff
        logit_grad = coef * (hot[0] - hot[1])
        high = logit_grad.astype(BF16)
        rest = logit_grad - high.astype(F32)
        mid = rest.astype(BF16)
        low = (rest - mid.astype(F32)).astype(BF16)
        cp_tok.wait()
        terms = jnp.dot(
            jnp.concatenate([high, mid, low], axis=0), tok[...], preferred_element_type=F32
        )
        term = terms[0:16] + terms[16:32] + terms[32:48]
        for p in range(16):
            rt[p] = term[(p // 8) * 8 : (p // 8) * 8 + 8, (p % 8) * 128 : (p % 8) * 128 + 128]

    def router_e():
        for k in range(1, NZ):
            to = (z + k) % NZ
            pltpu.make_async_remote_copy(
                src_ref=rt.at[to],
                dst_ref=r1.at[k - 1],
                send_sem=r_send.at[0],
                recv_sem=r_recv.at[0],
                device_id={"expert": to},
                device_id_type=MESH,
            ).start()

    def router_b():
        pltpu.make_async_copy(r1, r1, r_recv.at[0]).wait()
        total = rt[z]
        for k in range(NZ - 1):
            total = total + r1[k]
        r2[dp] = total
        for k in range(1, 2 * NY):
            pltpu.make_async_remote_copy(
                src_ref=r2.at[dp],
                dst_ref=r2.at[dp],
                send_sem=r_send.at[1],
                recv_sem=r_recv.at[1],
                device_id={"dp": (dp + k) % (2 * NY)},
                device_id_type=MESH,
            ).start()

    def router_c():
        pltpu.make_async_copy(r2.at[pl.ds(0, 7)], r2.at[pl.ds(0, 7)], r_recv.at[1]).wait()
        total = r2[0]
        for k in range(1, 2 * NY):
            total = total + r2[k]
        r3[z] = total
        for k in range(1, NZ):
            pltpu.make_async_remote_copy(
                src_ref=r3.at[z],
                dst_ref=r3.at[z],
                send_sem=r_send.at[2],
                recv_sem=r_recv.at[2],
                device_id={"expert": (z + k) % NZ},
                device_id_type=MESH,
            ).start()

    def router_d():
        pltpu.make_async_copy(r3.at[pl.ds(0, 15)], r3.at[pl.ds(0, 15)], r_recv.at[2]).wait()
        for p in range(16):
            rg_ref[(p // 8) * 8 : (p // 8) * 8 + 8, (p % 8) * 128 : (p % 8) * 128 + 128] = r3[p]

    def weights_here():
        for j in range(NJ):
            own, other = wbuf.at[j, pl.ds(0, HID)], wbuf.at[j, pl.ds(HID, HID)]
            pltpu.make_async_copy(own, own, w_sem.at[j]).wait()
            pltpu.make_async_copy(other, other, wr_sem.at[1, j]).wait()

    router_a()
    router_e()
    unpacked(0)
    unpacked(1)
    near(0)
    onward(0, OWN)
    unpacked(2)
    near(1)
    onward(1, OWN)
    across(0)
    onward(0, MINUS)
    onward(0, PLUS)
    unpacked(3)
    near(2)
    onward(2, OWN)
    across(1)
    onward(1, MINUS)
    onward(1, PLUS)
    onward(0, OPP)
    router_b()
    near(3)
    onward(3, OWN)
    across(2)
    onward(2, MINUS)
    onward(2, PLUS)
    onward(1, OPP)
    weights_here()
    matmul(0, OWN)
    across(3)
    onward(3, MINUS)
    onward(3, PLUS)
    router_c()
    matmul(0, MINUS)
    onward(2, OPP)
    matmul(0, PLUS)
    matmul(0, OPP)
    onward(3, OPP)
    matmul(1, OWN)
    matmul(1, MINUS)
    matmul(1, PLUS)
    finish(OWN)
    matmul(1, OPP)
    finish(MINUS)
    finish(PLUS)
    router_d()

    for j in range(NJ):
        pltpu.make_async_copy(tx.at[j, pl.ds(0, 31)], tx.at[j, pl.ds(0, 31)], z_send.at[j]).wait()
        sent = rows.at[j, pl.ds(0, 15)]
        pltpu.make_async_copy(sent, sent, a_send.at[j]).wait()
    for k in range(NX - 1):
        pltpu.make_async_copy(sc_tx, sc_tx, sc_send.at[k]).wait()
    pltpu.make_async_copy(r1, r1, r_send.at[0]).wait()
    pltpu.make_async_copy(r2.at[pl.ds(0, 7)], r2.at[pl.ds(0, 7)], r_send.at[1]).wait()
    pltpu.make_async_copy(r1, r1, r_send.at[2]).wait()
    for j in range(NJ):
        other = wbuf.at[j, pl.ds(HID, HID)]
        pltpu.make_async_copy(other, other, wr_sem.at[0, j]).wait()
    finish(OPP)
    for rel in range(NY):
        pltpu.make_async_copy(p_tx.at[rel], p_tx.at[rel], p_send.at[rel]).wait()


def body(
    grad_out,
    tokens_in,
    router_logits,
    expert_ids,
    slot_index,
    kept,
    expert_out,
    gate_pre,
    up_pre,
    down_weight,
):
    hbm = pl.BlockSpec(memory_space=pltpu.HBM)
    vmem = pl.BlockSpec(memory_space=pltpu.VMEM)
    dma = pltpu.SemaphoreType.DMA
    slots = gate_pre.shape[1]
    gate_grad, up_grad, router_grad = pl.pallas_call(
        kernel,
        out_shape=(
            jax.ShapeDtypeStruct((1, HID, slots), BF16),
            jax.ShapeDtypeStruct((1, HID, slots), BF16),
            jax.ShapeDtypeStruct((16, 1024), F32),
        ),
        in_specs=[hbm] * 10,
        out_specs=(vmem, vmem, vmem),
        scratch_shapes=[
            pltpu.VMEM((128, 1024), BF16),
            pltpu.VMEM((128, 1024), BF16),
            pltpu.VMEM((128, 2, 1024), BF16),
            pltpu.VMEM((HID, slots), BF16),
            pltpu.VMEM((HID, slots), BF16),
            pltpu.VMEM((16, 128), F32),
            pltpu.VMEM((2, 128), jnp.int32),
            pltpu.VMEM((2, 128), jnp.int32),
            pltpu.VMEM((2, 128), jnp.int32),
            pltpu.VMEM((NJ, 2 * HID, NX * PART), BF16),
            pltpu.VMEM((HID, slots), F32),
            pltpu.VMEM((HID, slots), F32),
            pltpu.VMEM((NJ, 2 * NZ, 16, 128), BF16),
            pltpu.VMEM((NJ, NZ, 16, 128), BF16),
            pltpu.VMEM((NJ, NZ, 16, 128), BF16),
            pltpu.VMEM((NJ, NY * NX, 2, PART // 2, 2 * ROWS), BF16),
            pltpu.VMEM((NY, HID, 2 * ROWS), F32),
            pltpu.VMEM((NY, HID, 2 * ROWS), F32),
            pltpu.VMEM((NY, HID, 2 * ROWS), F32),
            pltpu.VMEM((8, 128), F32),
            pltpu.VMEM((NX - 1, 8, 128), F32),
            pltpu.VMEM((NZ, 8, 128), F32),
            pltpu.VMEM((NZ - 1, 8, 128), F32),
            pltpu.VMEM((2 * NY, 8, 128), F32),
            pltpu.VMEM((NZ, 8, 128), F32),
            dma((9,)),
            dma((NJ,)),
            dma((2, NJ)),
            dma((NJ,)),
            dma((NJ, 2)),
            dma((NJ,)),
            dma((2, 2, NJ, 20)),
            dma((NY,)),
            dma((NY,)),
            dma((NX - 1,)),
            dma((NX - 1,)),
            dma((3,)),
            dma((3,)),
        ],
        compiler_params=pltpu.CompilerParams(
            collective_id=0, has_side_effects=True, vmem_limit_bytes=24 * 1024 * 1024
        ),
    )(
        *(
            pltpu.with_memory_space_constraint(arg, pltpu.HBM)
            for arg in (
                grad_out,
                tokens_in,
                expert_out,
                jnp.swapaxes(gate_pre, 1, 2),
                jnp.swapaxes(up_pre, 1, 2),
                down_weight,
                router_logits.T,
                expert_ids.T,
                slot_index.T,
                kept.T,
            )
        )
    )
    return jnp.swapaxes(gate_grad, 1, 2), jnp.swapaxes(up_grad, 1, 2), router_grad


def solution(mesh):
    in_specs = (
        P(("dp", "expert"), "tensor"),
        P(("dp", "expert"), "tensor"),
        P(("dp", "expert"), None),
        P(("dp", "expert"), None),
        P(("dp", "expert"), None),
        P(("dp", "expert"), None),
        P(("dp", "expert"), None, "tensor"),
        P("expert", None, ("dp", "tensor")),
        P("expert", None, ("dp", "tensor")),
        P("expert", ("dp", "tensor"), None),
    )
    out_specs = (
        P("expert", None, ("dp", "tensor")),
        P("expert", None, ("dp", "tensor")),
        P(None, "tensor"),
    )
    return jax.shard_map(body, mesh=mesh, in_specs=in_specs, out_specs=out_specs, check_vma=False)
```
